512 devices in a mesh: row: 16 (over y, core), col: 32 (over z, x).
Axes of the slice: x: 4, y: 8, z: 8, core: 2. Of those that a mesh axis runs over, the one named last changes fastest.
Arguments:
- tokens: bfloat16 [256, 12288], P('col', 'row'), may hold values from -6 to 6
- up_weight: bfloat16 [12288, 24576], P('row', 'col'), may hold values from -0.0546875 to 0.0546875
- down_weight: bfloat16 [24576, 12288], P('col', 'row'), may hold values from -0.0390625 to 0.0390625
- cotangent: bfloat16 [256, 12288], P('col', 'row'), may hold values from -1.5 to 1.5
Outputs:
- layer_out: bfloat16 [256, 12288], P('col', 'row')
- input_grad: bfloat16 [256, 12288], P('col', 'row')
- up_grad: bfloat16 [12288, 24576], P('row', 'col')
- down_grad: bfloat16 [24576, 12288], P('col', 'row')
The draws below stay inside these ranges and needn't reach their ends.
All inputs are finite; a program needn't handle non-finite values.
Results may differ from the reference program's by a relative error of at most 0.005.
Values may be sent and summed in bfloat16 or wider, within the bound.
A program may use at most 64 MiB of HBM per device.

```python
import math
import jax
import jax.numpy as jnp

D = 12288
FF = 24576
TOKENS = 256


def steps_of(key, dims, pieces, low, largest):
    factor_of = 1.0
    for axis_at, parts in pieces:
        steps = jax.random.uniform(jax.random.fold_in(jax.random.fold_in(key, 6), axis_at), (parts,), jnp.float32, low / len(pieces), largest / len(pieces))
        factor_of = factor_of * jnp.repeat(jnp.exp(steps), dims[axis_at] // parts).reshape((-1,) + (1,) * (len(dims) - 1 - axis_at))
    return factor_of


def bell_draw(own_key, dims, spread, most, pieces=(), kind=jnp.bfloat16):
    array = jax.random.normal(own_key, dims, jnp.float32) * spread
    if len(pieces) > 0:
        array = steps_of(own_key, dims, pieces, -0.22, 0.18) * array
    return jnp.clip(array, min=-most, max=most).astype(kind)


def setup_inputs(seed: int = 0) -> dict:
    splits = jax.random.split(jax.random.key(seed), 5)
    return {
        "tokens": bell_draw(splits[0], (TOKENS, D), 1.0, 6.0, ((0, 32), (1, 16))),
        "up_weight": bell_draw(splits[1], (D, FF), D ** -0.5, 0.0546875, ((0, 16), (1, 32))),
        "down_weight": bell_draw(splits[2], (FF, D), FF ** -0.5, 0.0390625, ((0, 32), (1, 16))),
        "cotangent": bell_draw(splits[3], (TOKENS, D), 0.25, 1.5, ((0, 32), (1, 16))),
    }


coeff_cubic = 0.044715
root_ratio = math.sqrt(2.0 / math.pi)

def gelu_parts(preact):
    inner = jnp.tanh(root_ratio * (preact + coeff_cubic * preact * preact * preact))
    values = 0.5 * preact * (1.0 + inner)
    slopes = 0.5 * (1.0 + inner) + 0.5 * preact * (1.0 - inner * inner) * root_ratio * (1.0 + 3.0 * coeff_cubic * preact * preact)
    return (values, slopes)

def reference(tokens, up_weight, down_weight, cotangent):
    preact = jnp.dot(tokens, up_weight, preferred_element_type=jnp.float32)
    hidden_back = jnp.dot(cotangent, down_weight.T, preferred_element_type=jnp.float32)
    values, slopes = gelu_parts(preact)
    activated = values.astype(jnp.bfloat16)
    hidden_grad = (hidden_back * slopes).astype(jnp.bfloat16)
    layer_out = jnp.dot(activated, down_weight, preferred_element_type=jnp.float32).astype(jnp.bfloat16)
    input_grad = jnp.dot(hidden_grad, up_weight.T, preferred_element_type=jnp.float32).astype(jnp.bfloat16)
    up_grad = jnp.dot(tokens.T, hidden_grad, preferred_element_type=jnp.float32).astype(jnp.bfloat16)
    down_grad = jnp.dot(activated.T, cotangent, preferred_element_type=jnp.float32).astype(jnp.bfloat16)
    return (layer_out, input_grad, up_grad, down_grad)
```

```python
import math

import jax
import jax.numpy as jnp
from jax import lax
from jax.experimental import pallas as pl
from jax.experimental.pallas import tpu as pltpu
from jax.sharding import PartitionSpec as P

coeff_cubic = 0.044715
root_ratio = math.sqrt(2.0 / math.pi)
MESH = pl.DeviceIdType.MESH
BF = jnp.bfloat16
F32 = jnp.float32

NY, NK, NZ, NX = 8, 2, 8, 4
NEAR = (1, 7, 2, 6, 3, 5, 4)
FAR = (4, 3, 5, 2, 6, 1, 7)


def gelu_parts(preact):
    inner = jnp.tanh(root_ratio * (preact + coeff_cubic * preact * preact * preact))
    values = 0.5 * preact * (1.0 + inner)
    slopes = 0.5 * (1.0 + inner) + 0.5 * preact * (1.0 - inner * inner) * root_ratio * (
        1.0 + 3.0 * coeff_cubic * preact * preact
    )
    return (values, slopes)


def dot(left, right, dims):
    return lax.dot_general(left, right, (dims, ((), ())), preferred_element_type=F32)


NN = ((1,), (0,))
NT = ((1,), (1,))
TN = ((0,), (0,))


def kernel(
    tok_ref, cot_ref, up_hbm, down_hbm,
    lo_ref, ig_ref, ug_hbm, dg_hbm,
    up, down, ug, dg,
    gat, xs, cs,
    part, pair, send_b, recv_b,
    ah, prod, send_x, recv_x, send_z, recv_z,
    wsem, gsem,
    az_s, ax_s, a_r,
    p_s, p_r,
    b_s, b_r,
    c_s, cf_s, c_r,
    dx_s, dx_r, dz_s, dz_r,
):
    w = up.shape[0]
    h = up.shape[1]
    row = lax.axis_index("row")
    col = lax.axis_index("col")
    y, k = row // NK, row % NK
    z, x = col // NX, col % NX

    def at_y(d):
        return (lax.rem(y + d, NY) * NK + k, col)

    def at_z(d):
        return (row, lax.rem(z + d, NZ) * NX + x)

    def at_x(d):
        return (row, z * NX + lax.rem(x + d, NX))

    other = (y * NK + 1 - k, col)

    def copy(src, dst, ss, rs, device):
        return pltpu.make_async_remote_copy(
            src_ref=src, dst_ref=dst, send_sem=ss, recv_sem=rs, device_id=device, device_id_type=MESH
        )

    load_up = pltpu.make_async_copy(up_hbm, up, wsem.at[0])
    load_down = pltpu.make_async_copy(down_hbm, down, wsem.at[1])
    load_up.start()
    load_down.start()

    barrier = pltpu.get_barrier_semaphore()
    peers = [at_y(d) for d in FAR] + [at_z(d) for d in FAR] + [at_x(d) for d in (2, 1, 3)] + [other]
    for device in peers:
        pl.semaphore_signal(barrier, inc=1, device_id=device, device_id_type=MESH)
    gat[col] = jnp.concatenate([tok_ref[...].astype(F32), cot_ref[...].astype(F32)], axis=0).astype(BF)
    pl.semaphore_wait(barrier, len(peers))

    pending = []
    for d in FAR:
        c = copy(gat.at[col], gat.at[col], az_s.at[d], a_r.at[col], at_z(d))
        c.start()
        pending.append(c)
    for s in (0,) + NEAR:
        slot = lax.rem(z + s, NZ) * NX + x
        if s:
            copy(gat.at[slot], gat.at[slot], az_s.at[0], a_r.at[slot], at_z(s)).wait_recv()
        for d in (2, 1, 3):
            c = copy(gat.at[slot], gat.at[slot], ax_s.at[s * NX + d], a_r.at[slot], at_x(d))
            c.start()
            pending.append(c)
    for s in (0,) + NEAR:
        zz = lax.rem(z + s, NZ)
        for d in (1, 3, 2):
            slot = zz * NX + lax.rem(x + d, NX)
            copy(gat.at[slot], gat.at[slot], az_s.at[0], a_r.at[slot], at_x(d)).wait_recv()
        blocks = [gat[zz * NX + i].astype(F32) for i in range(NX)]
        rows = pl.ds(pl.multiple_of(zz * 32, 32), 32)
        xs[rows, :] = jnp.concatenate([b[:8] for b in blocks], axis=0).astype(BF)
        cs[rows, :] = jnp.concatenate([b[8:] for b in blocks], axis=0).astype(BF)
    for c in pending:
        c.wait_send()

    load_up.wait()
    load_down.wait()
    part[:, :h] = dot(xs[...], up[...], NN)
    part[:, h:] = dot(cs[...], down[...], NT)

    mine = pl.ds(pl.multiple_of(k * 128, 128), 128)
    theirs = pl.ds(pl.multiple_of((1 - k) * 128, 128), 128)
    c = copy(part.at[theirs], pair, p_s, p_r, other)
    c.start()
    c.wait()
    pair[...] = pair[...] + part[mine, :]
    for b in range(NY):
        send_b[b] = pair[pl.ds(b * 16, 16), :].astype(BF)
    pending = []
    for d in FAR:
        to = lax.rem(y + d, NY)
        c = copy(send_b.at[to], recv_b.at[y], b_s.at[d], b_r.at[y], at_y(d))
        c.start()
        pending.append(c)
    total = pair[pl.ds(pl.multiple_of(y * 16, 16), 16), :]
    for s in NEAR:
        slot = lax.rem(y + s, NY)
        copy(recv_b.at[slot], recv_b.at[slot], b_s.at[0], b_r.at[slot], at_y(s)).wait_recv()
        total = total + recv_b[slot].astype(F32)
    for c in pending:
        c.wait_send()

    values, slopes = gelu_parts(total[:, :h])
    own = k * NY + y
    ah[own] = jnp.concatenate([values, total[:, h:] * slopes], axis=1).astype(BF)

    pending = []
    for d in FAR:
        c = copy(ah.at[own], ah.at[own], c_s.at[d], c_r.at[own], at_y(d))
        c.start()
        pending.append(c)
    for s in (0,) + NEAR:
        slot = k * NY + lax.rem(y + s, NY)
        if s:
            copy(ah.at[slot], ah.at[slot], c_s.at[0], c_r.at[slot], at_y(s)).wait_recv()
        c = copy(ah.at[slot], ah.at[slot], cf_s.at[s], c_r.at[slot], other)
        c.start()
        pending.append(c)
    for s in (0,) + NEAR:
        slot = (1 - k) * NY + lax.rem(y + s, NY)
        copy(ah.at[slot], ah.at[slot], c_s.at[0], c_r.at[slot], other).wait_recv()
    for c in pending:
        c.wait_send()

    prod[:, :w] = dot(ah[:, :, :h].reshape(256, h), down[...], NN)
    prod[:, w:] = dot(ah[:, :, h:].reshape(256, h), up[...], NT)

    pending = []
    for d in FAR + (0,):
        zz = lax.rem(z + d, NZ)
        for e in (2, 1, 3):
            to = lax.rem(x + e, NX)
            rows = pl.ds(pl.multiple_of(zz * 32 + to * 8, 8), 8)
            send_x[zz * NX + to] = jnp.concatenate([prod[rows, :w], prod[rows, w:]], axis=0).astype(BF)
            c = copy(
                send_x.at[zz * NX + to], recv_x.at[zz * NX + x],
                dx_s.at[d * NX + e], dx_r.at[zz * NX + x], at_x(e),
            )
            c.start()
            pending.append(c)

    ug[...] = dot(xs[...], ah[:, :, h:].reshape(256, h), TN).astype(BF)
    store_up = pltpu.make_async_copy(ug, ug_hbm, gsem.at[0])
    store_up.start()
    dg[...] = dot(ah[:, :, :h].reshape(256, h), cs[...], TN).astype(BF)
    store_down = pltpu.make_async_copy(dg, dg_hbm, gsem.at[1])
    store_down.start()

    for d in FAR + (0,):
        zz = lax.rem(z + d, NZ)
        rows = pl.ds(pl.multiple_of(zz * 32 + x * 8, 8), 8)
        total = jnp.concatenate([prod[rows, :w], prod[rows, w:]], axis=0)
        for e in (1, 3, 2):
            slot = zz * NX + lax.rem(x + e, NX)
            copy(recv_x.at[slot], recv_x.at[slot], dx_s.at[0], dx_r.at[slot], at_x(e)).wait_recv()
            total = total + recv_x[slot].astype(F32)
        if d:
            send_z[zz] = total.astype(BF)
            c = copy(send_z.at[zz], recv_z.at[z], dz_s.at[d], dz_r.at[z], at_z(d))
            c.start()
            pending.append(c)
    for s in NEAR:
        slot = lax.rem(z + s, NZ)
        copy(recv_z.at[slot], recv_z.at[slot], dz_s.at[0], dz_r.at[slot], at_z(s)).wait_recv()
        total = total + recv_z[slot].astype(F32)
    lo_ref[...] = total[:8].astype(BF)
    ig_ref[...] = total[8:].astype(BF)
    for c in pending:
        c.wait_send()
    store_up.wait()
    store_down.wait()


def local(tokens, up_weight, down_weight, cotangent):
    w, h = up_weight.shape
    dma = pltpu.SemaphoreType.DMA
    vmem = pl.BlockSpec(memory_space=pltpu.VMEM)
    hbm = pl.BlockSpec(memory_space=pl.ANY)
    lo, ig, ug, dg = pl.pallas_call(
        kernel,
        out_shape=(
            jax.ShapeDtypeStruct((8, w), BF),
            jax.ShapeDtypeStruct((8, w), BF),
            jax.ShapeDtypeStruct((w, h), BF),
            jax.ShapeDtypeStruct((h, w), BF),
        ),
        in_specs=[vmem, vmem, hbm, hbm],
        out_specs=(vmem, vmem, hbm, hbm),
        scratch_shapes=[
            pltpu.VMEM((w, h), BF), pltpu.VMEM((h, w), BF), pltpu.VMEM((w, h), BF), pltpu.VMEM((h, w), BF),
            pltpu.VMEM((32, 16, w), BF), pltpu.VMEM((256, w), BF), pltpu.VMEM((256, w), BF),
            pltpu.VMEM((256, 2 * h), F32), pltpu.VMEM((128, 2 * h), F32),
            pltpu.VMEM((NY, 16, 2 * h), BF), pltpu.VMEM((NY, 16, 2 * h), BF),
            pltpu.VMEM((16, 16, 2 * h), BF), pltpu.VMEM((256, 2 * w), F32),
            pltpu.VMEM((32, 16, w), BF), pltpu.VMEM((32, 16, w), BF),
            pltpu.VMEM((NZ, 16, w), BF), pltpu.VMEM((NZ, 16, w), BF),
            dma((2,)), dma((2,)),
            dma((NZ,)), dma((NZ * NX,)), dma((NZ * NX,)),
            dma, dma,
            dma((NY,)), dma((NY,)),
            dma((NY,)), dma((NY,)), dma((2 * NY,)),
            dma((NZ * NX,)), dma((NZ * NX,)), dma((NZ,)), dma((NZ,)),
        ],
        compiler_params=pltpu.CompilerParams(
            collective_id=0, has_side_effects=True, vmem_limit_bytes=48 << 20
        ),
        cost_estimate=pl.CostEstimate(flops=1812000000, bytes_accessed=4800000, transcendentals=12288),
        name="sublayer",
    )(tokens, cotangent, up_weight, down_weight)
    return lo, ig, ug, dg


def solution(mesh):
    in_specs = (P("col", "row"), P("row", "col"), P("col", "row"), P("col", "row"))
    out_specs = (P("col", "row"), P("col", "row"), P("row", "col"), P("col", "row"))
    return jax.shard_map(local, mesh=mesh, in_specs=in_specs, out_specs=out_specs, check_vma=False)
```

```python
import math

import jax
import jax.numpy as jnp
from jax import lax
from jax.experimental import pallas as pl
from jax.experimental.pallas import tpu as pltpu
from jax.sharding import PartitionSpec as P

coeff_cubic = 0.044715
root_ratio = math.sqrt(2.0 / math.pi)
MESH = pl.DeviceIdType.MESH
BF = jnp.bfloat16
F32 = jnp.float32

NY, NK, NZ, NX = 8, 2, 8, 4
NEAR = (1, 7, 2, 6, 3, 5, 4)
FAR = (4, 3, 5, 2, 6, 1, 7)


def gelu_parts(preact):
    inner = jnp.tanh(root_ratio * (preact + coeff_cubic * preact * preact * preact))
    values = 0.5 * preact * (1.0 + inner)
    slopes = 0.5 * (1.0 + inner) + 0.5 * preact * (1.0 - inner * inner) * root_ratio * (
        1.0 + 3.0 * coeff_cubic * preact * preact
    )
    return (values, slopes)


def dot(left, right, dims):
    return lax.dot_general(left, right, (dims, ((), ())), preferred_element_type=F32)


NN = ((1,), (0,))
NT = ((1,), (1,))
TN = ((0,), (0,))


def fold(block):
    half = block.shape[1] // 2
    return jnp.concatenate([block[:, :half], block[:, half:]], axis=0)


def unfold(block):
    return jnp.concatenate([block[:8], block[8:]], axis=1)


def kernel(
    tok_hbm, cot_hbm, up_hbm, down_hbm,
    lo_ref, ig_ref, ug_ref, dg_ref,
    up, down, shard, gat, xs, part, pair, send_b, recv_b, ah, prod, send_x, recv_x, send_z, recv_z,
    wsem, az_s, az_r, ax_s, ax_r, p_s, p_r, b_s, b_r, c_s, c_r, f_s, f_r, dx_s, dx_r, dz_s, dz_r,
):
    row = lax.axis_index("row")
    col = lax.axis_index("col")
    y, k = row // NK, row % NK
    z, x = col // NX, col % NX

    def at_y(d):
        return (lax.rem(y + d, NY) * NK + k, col)

    def at_z(d):
        return (row, lax.rem(z + d, NZ) * NX + x)

    def at_x(d):
        return (row, z * NX + lax.rem(x + d, NX))

    other = (y * NK + 1 - k, col)
    pending = []

    def copy(src, dst, ss, rs, device):
        return pltpu.make_async_remote_copy(
            src_ref=src, dst_ref=dst, send_sem=ss, recv_sem=rs, device_id=device, device_id_type=MESH
        )

    def send(src, dst, ss, rs, device):
        c = copy(src, dst, ss, rs, device)
        c.start()
        pending.append(c)

    def arrived(dst, ss, rs, device):
        copy(dst, dst, ss, rs, device).wait_recv()

    load_tok = pltpu.make_async_copy(tok_hbm, shard.at[0], wsem.at[0])
    load_cot = pltpu.make_async_copy(cot_hbm, shard.at[1], wsem.at[1])
    load_up = pltpu.make_async_copy(up_hbm, up, wsem.at[2])
    load_down = pltpu.make_async_copy(down_hbm, down, wsem.at[3])
    load_tok.start()
    load_cot.start()
    load_up.start()
    load_down.start()

    barrier = pltpu.get_barrier_semaphore()
    peers = [at_y(d) for d in FAR] + [at_z(d) for d in FAR] + [at_x(d) for d in (2, 1, 3)] + [other]
    for device in peers:
        pl.semaphore_signal(barrier, inc=1, device_id=device, device_id_type=MESH)
    load_tok.wait()
    load_cot.wait()
    for n in (0, 1):
        gat[n, x, z] = fold(shard[n].astype(F32)).astype(BF)
    pl.semaphore_wait(barrier, len(peers))

    for n in (0, 1):
        for d in FAR:
            send(gat.at[n, x, z], gat.at[n, x, z], az_s.at[n, d], az_r.at[n, z], at_z(d))
    for n in (0, 1):
        for s in (0, 1, 3, 2):
            p = lax.rem(z // 2 + s, NZ // 2)
            if s == 0:
                mate = z + 1 - 2 * lax.rem(z, 2)
                arrived(gat.at[n, x, mate], az_s.at[n, 0], az_r.at[n, mate], at_z(1))
            else:
                for i in (0, 1):
                    arrived(gat.at[n, x, 2 * p + i], az_s.at[n, 0], az_r.at[n, 2 * p + i], at_z(1))
            for d in (2, 1, 3):
                block = gat.at[n, x, pl.ds(2 * p, 2)]
                send(block, block, ax_s.at[n, s, d], ax_r.at[n, x, p], at_x(d))
    for n in (0, 1):
        for s in (0, 1, 3, 2):
            p = lax.rem(z // 2 + s, NZ // 2)
            for d in (1, 3, 2):
                xx = lax.rem(x + d, NX)
                arrived(gat.at[n, xx, pl.ds(2 * p, 2)], ax_s.at[n, 0, 0], ax_r.at[n, xx, p], at_x(d))
            blocks = [unfold(gat[n, j, 2 * p + i].astype(F32)) for i in (0, 1) for j in range(NX)]
            xs[n, pl.ds(pl.multiple_of(p * 64, 64), 64), :] = jnp.concatenate(blocks, axis=0).astype(BF)

        mine = pl.ds(pl.multiple_of(k * 128, 128), 128)
        theirs = pl.ds(pl.multiple_of((1 - k) * 128, 128), 128)
        if n == 0:
            load_up.wait()
        else:
            load_down.wait()
        weight, dims = ((up, NN), (down, NT))[n]
        part[n, 0] = dot(xs[n, theirs, :], weight[...], dims)
        send(part.at[n, 0], pair.at[n], p_s.at[n], p_r.at[n], other)
        part[n, 1] = dot(xs[n, mine, :], weight[...], dims)

    for n in (0, 1):
        arrived(pair.at[n], p_s.at[n], p_r.at[n], other)
        for d in FAR + (0,):
            to = lax.rem(y + d, NY)
            rows = pl.ds(pl.multiple_of(to * 16, 16), 16)
            total = part[n, 1, rows, :] + pair[n, rows, :]
            if d:
                send_b[n, to] = total.astype(BF)
                send(send_b.at[n, to], recv_b.at[n, y], b_s.at[n, d], b_r.at[n, y], at_y(d))
            else:
                part[n, 1, rows, :] = total
    own = pl.ds(pl.multiple_of(y * 16, 16), 16)
    at = k * NY + y
    for n in (0, 1):
        total = part[n, 1, own, :]
        for s in NEAR:
            slot = lax.rem(y + s, NY)
            arrived(recv_b.at[n, slot], b_s.at[n, 0], b_r.at[n, slot], at_y(s))
            total = total + recv_b[n, slot].astype(F32)
        if n == 0:
            values, slopes = gelu_parts(total)
            ah[0, at] = values.astype(BF)
        else:
            ah[1, at] = (total * slopes).astype(BF)
        for d in FAR:
            send(ah.at[n, at], ah.at[n, at], c_s.at[n, d], c_r.at[n, y], at_y(d))
        send(ah.at[n, at], ah.at[n, at], f_s.at[n, 0], f_r.at[n, y], other)
    for n in (0, 1):
        for s in NEAR:
            yy = lax.rem(y + s, NY)
            block = ah.at[n, k * NY + yy]
            arrived(block, c_s.at[n, 0], c_r.at[n, yy], at_y(s))
            send(block, block, f_s.at[n, s], f_r.at[n, yy], other)
        for s in (0,) + NEAR:
            yy = lax.rem(y + s, NY)
            arrived(ah.at[n, (1 - k) * NY + yy], f_s.at[n, 0], f_r.at[n, yy], other)
        weight, dims = ((down, NN), (up, NT))[n]
        prod[n] = dot(ah[n].reshape(256, ah.shape[3]), weight[...], dims)
        for s in (2, 1, 3, 0):
            p = lax.rem(z // 2 + s, NZ // 2)
            for e in (2, 1, 3):
                to = lax.rem(x + e, NX)
                for i in (0, 1):
                    rows = pl.ds(pl.multiple_of(p * 64 + i * 32 + to * 8, 8), 8)
                    send_x[n, to, 2 * p + i] = fold(prod[n, rows, :]).astype(BF)
                send(
                    send_x.at[n, to, pl.ds(2 * p, 2)], recv_x.at[n, x, pl.ds(2 * p, 2)],
                    dx_s.at[n, s, e], dx_r.at[n, x, p], at_x(e),
                )

    totals = []
    for n in (0, 1):
        for s in (2, 1, 3, 0):
            p = lax.rem(z // 2 + s, NZ // 2)
            for e in (1, 3, 2):
                xx = lax.rem(x + e, NX)
                arrived(recv_x.at[n, xx, pl.ds(2 * p, 2)], dx_s.at[n, 0, 0], dx_r.at[n, xx, p], at_x(e))
            for i in (0, 1):
                zz = 2 * p + i if s else (z + 1 - 2 * lax.rem(z, 2), z)[i]
                rows = pl.ds(pl.multiple_of(zz * 32 + x * 8, 8), 8)
                total = fold(prod[n, rows, :])
                for e in (1, 3, 2):
                    total = total + recv_x[n, lax.rem(x + e, NX), zz].astype(F32)
                if s or i == 0:
                    send_z[n, zz] = total.astype(BF)
                    send(send_z.at[n, zz], recv_z.at[n, z], dz_s.at[n, 2 * s + i], dz_r.at[n, z], (row, zz * NX + x))
        totals.append(total)
        if n == 0:
            ug_ref[...] = dot(xs[0], ah[1].reshape(256, ah.shape[3]), TN).astype(BF)
            dg_ref[...] = dot(ah[0].reshape(256, ah.shape[3]), xs[1], TN).astype(BF)
    for n in (0, 1):
        total = totals[n]
        for s in NEAR:
            slot = lax.rem(z + s, NZ)
            arrived(recv_z.at[n, slot], dz_s.at[n, 0], dz_r.at[n, slot], at_z(s))
            total = total + recv_z[n, slot].astype(F32)
        (lo_ref, ig_ref)[n][...] = unfold(total).astype(BF)
    for c in pending:
        c.wait_send()


def store(a, b, c, d, a_out, b_out, c_out, d_out, sems):
    copies = [
        pltpu.make_async_copy(src, dst, sems.at[i])
        for i, (src, dst) in enumerate(((c, c_out), (d, d_out), (a, a_out), (b, b_out)))
    ]
    for c in copies:
        c.start()
    for c in copies:
        c.wait()


def local(tokens, up_weight, down_weight, cotangent):
    w, h = up_weight.shape
    dma = pltpu.SemaphoreType.DMA
    vmem = pl.BlockSpec(memory_space=pltpu.VMEM)
    hbm = pl.BlockSpec(memory_space=pltpu.HBM)
    shapes = (
        jax.ShapeDtypeStruct((8, w), BF),
        jax.ShapeDtypeStruct((8, w), BF),
        jax.ShapeDtypeStruct((w, h), BF),
        jax.ShapeDtypeStruct((h, w), BF),
    )
    results = pl.pallas_call(
        kernel,
        out_shape=shapes,
        in_specs=[hbm] * 4,
        out_specs=(vmem,) * 4,
        scratch_shapes=[
            pltpu.VMEM((w, h), BF), pltpu.VMEM((h, w), BF),
            pltpu.VMEM((2, 8, w), BF),
            pltpu.VMEM((2, NX, NZ, 16, w // 2), BF),
            pltpu.VMEM((2, 256, w), BF),
            pltpu.VMEM((2, 2, 128, h), F32), pltpu.VMEM((2, 128, h), F32),
            pltpu.VMEM((2, NY, 16, h), BF), pltpu.VMEM((2, NY, 16, h), BF),
            pltpu.VMEM((2, 16, 16, h), BF),
            pltpu.VMEM((2, 256, w), F32),
            pltpu.VMEM((2, NX, NZ, 16, w // 2), BF), pltpu.VMEM((2, NX, NZ, 16, w // 2), BF),
            pltpu.VMEM((2, NZ, 16, w // 2), BF), pltpu.VMEM((2, NZ, 16, w // 2), BF),
            dma((4,)),
            dma((2, NZ)), dma((2, NZ)), dma((2, 4, NX)), dma((2, NX, 4)),
            dma((2,)), dma((2,)),
            dma((2, NY)), dma((2, NY)),
            dma((2, NY)), dma((2, NY)), dma((2, NY)), dma((2, NY)),
            dma((2, 4, NX)), dma((2, NX, 4)), dma((2, NZ)), dma((2, NZ)),
        ],
        compiler_params=pltpu.CompilerParams(
            collective_id=0, has_side_effects=True, vmem_limit_bytes=40 << 20
        ),
        cost_estimate=pl.CostEstimate(flops=1812000000, bytes_accessed=4800000, transcendentals=12288),
        name="sublayer",
    )(*(pltpu.with_memory_space_constraint(a, pltpu.HBM) for a in (tokens, cotangent, up_weight, down_weight)))
    return pl.pallas_call(
        store,
        out_shape=shapes,
        in_specs=[pl.BlockSpec(memory_space=pl.ANY)] * 4,
        out_specs=(hbm,) * 4,
        scratch_shapes=[dma((4,))],
        name="store",
    )(*results)


def solution(mesh):
    in_specs = (P("col", "row"), P("row", "col"), P("col", "row"), P("col", "row"))
    out_specs = (P("col", "row"), P("col", "row"), P("row", "col"), P("col", "row"))
    return jax.shard_map(local, mesh=mesh, in_specs=in_specs, out_specs=out_specs, check_vma=False)
```

```python
import math

import jax
import jax.numpy as jnp
from jax import lax
from jax.experimental import pallas as pl
from jax.experimental.pallas import tpu as pltpu
from jax.sharding import PartitionSpec as P

coeff_cubic = 0.044715
root_ratio = math.sqrt(2.0 / math.pi)
MESH = pl.DeviceIdType.MESH
BF = jnp.bfloat16
F32 = jnp.float32

NY, NK, NZ, NX = 8, 2, 8, 4
NEAR = (1, 7, 2, 6, 3, 5, 4)
FAR = (4, 3, 5, 2, 6, 1, 7)


def gelu_parts(preact):
    inner = jnp.tanh(root_ratio * (preact + coeff_cubic * preact * preact * preact))
    values = 0.5 * preact * (1.0 + inner)
    slopes = 0.5 * (1.0 + inner) + 0.5 * preact * (1.0 - inner * inner) * root_ratio * (
        1.0 + 3.0 * coeff_cubic * preact * preact
    )
    return (values, slopes)


def dot(left, right, dims):
    return lax.dot_general(left, right, (dims, ((), ())), preferred_element_type=F32)


NN = ((1,), (0,))
NT = ((1,), (1,))
TN = ((0,), (0,))


def fold(block):
    half = block.shape[1] // 2
    return jnp.concatenate([block[:, :half], block[:, half:]], axis=0)


def unfold(block):
    return jnp.concatenate([block[:8], block[8:]], axis=1)


def kernel(
    tok_hbm, cot_hbm, up_hbm, down_hbm,
    lo_ref, ig_ref, ug_ref, dg_ref,
    up, down, shard, gat, xs, part, pair, send_b, recv_b, ah, prod, send_x, recv_x, send_z, recv_z,
    wsem, az_s, az_r, ax_s, ax_r, p_s, p_r, b_s, b_r, c_s, c_r, f_s, f_r, dx_s, dx_r, dz_s, dz_r,
):
    row = lax.axis_index("row")
    col = lax.axis_index("col")
    y, k = row // NK, row % NK
    z, x = col // NX, col % NX

    def at_y(d):
        return (lax.rem(y + d, NY) * NK + k, col)

    def at_z(d):
        return (row, lax.rem(z + d, NZ) * NX + x)

    def at_x(d):
        return (row, z * NX + lax.rem(x + d, NX))

    other = (y * NK + 1 - k, col)
    pending = []

    def copy(src, dst, ss, rs, device):
        return pltpu.make_async_remote_copy(
            src_ref=src, dst_ref=dst, send_sem=ss, recv_sem=rs, device_id=device, device_id_type=MESH
        )

    def send(src, dst, ss, rs, device):
        c = copy(src, dst, ss, rs, device)
        c.start()
        pending.append(c)

    def arrived(dst, ss, rs, device):
        copy(dst, dst, ss, rs, device).wait_recv()

    load_tok = pltpu.make_async_copy(tok_hbm, shard.at[0], wsem.at[0])
    load_cot = pltpu.make_async_copy(cot_hbm, shard.at[1], wsem.at[1])
    load_up = pltpu.make_async_copy(up_hbm, up, wsem.at[2])
    load_down = pltpu.make_async_copy(down_hbm, down, wsem.at[3])
    load_tok.start()
    load_cot.start()
    load_up.start()
    load_down.start()

    barrier = pltpu.get_barrier_semaphore()
    peers = [at_y(d) for d in FAR] + [at_z(d) for d in FAR] + [at_x(d) for d in (2, 1, 3)] + [other]
    for device in peers:
        pl.semaphore_signal(barrier, inc=1, device_id=device, device_id_type=MESH)
    load_tok.wait()
    load_cot.wait()
    for n in (0, 1):
        gat[n, x, z] = fold(shard[n].astype(F32)).astype(BF)
    pl.semaphore_wait(barrier, len(peers))

    for n in (0, 1):
        for d in FAR:
            send(gat.at[n, x, z], gat.at[n, x, z], az_s.at[n, d], az_r.at[n, z], at_z(d))
    for n in (0, 1):
        for s in (0, 1, 3, 2):
            p = lax.rem(z // 2 + s, NZ // 2)
            if s == 0:
                mate = z + 1 - 2 * lax.rem(z, 2)
                arrived(gat.at[n, x, mate], az_s.at[n, 0], az_r.at[n, mate], at_z(1))
            else:
                for i in (0, 1):
                    arrived(gat.at[n, x, 2 * p + i], az_s.at[n, 0], az_r.at[n, 2 * p + i], at_z(1))
            for d in (2, 1, 3):
                block = gat.at[n, x, pl.ds(2 * p, 2)]
                send(block, block, ax_s.at[n, s, d], ax_r.at[n, x, p], at_x(d))
    for n in (0, 1):
        for s in (0, 1, 3, 2):
            p = lax.rem(z // 2 + s, NZ // 2)
            for d in (1, 3, 2):
                xx = lax.rem(x + d, NX)
                arrived(gat.at[n, xx, pl.ds(2 * p, 2)], ax_s.at[n, 0, 0], ax_r.at[n, xx, p], at_x(d))
            blocks = [unfold(gat[n, j, 2 * p + i].astype(F32)) for i in (0, 1) for j in range(NX)]
            xs[n, pl.ds(pl.multiple_of(p * 64, 64), 64), :] = jnp.concatenate(blocks, axis=0).astype(BF)

        mine = pl.ds(pl.multiple_of(k * 128, 128), 128)
        theirs = pl.ds(pl.multiple_of((1 - k) * 128, 128), 128)
        if n == 0:
            load_up.wait()
        else:
            load_down.wait()
        weight, dims = ((up, NN), (down, NT))[n]
        part[n, 0] = dot(xs[n, theirs, :], weight[...], dims)
        send(part.at[n, 0], pair.at[n], p_s.at[n], p_r.at[n], other)
        part[n, 1] = dot(xs[n, mine, :], weight[...], dims)

    for n in (0, 1):
        arrived(pair.at[n], p_s.at[n], p_r.at[n], other)
        for d in FAR + (0,):
            to = lax.rem(y + d, NY)
            rows = pl.ds(pl.multiple_of(to * 16, 16), 16)
            total = part[n, 1, rows, :] + pair[n, rows, :]
            if d:
                send_b[n, to] = total.astype(BF)
                send(send_b.at[n, to], recv_b.at[n, y], b_s.at[n, d], b_r.at[n, y], at_y(d))
            else:
                part[n, 1, rows, :] = total
    own = pl.ds(pl.multiple_of(y * 16, 16), 16)
    at = k * NY + y
    for n in (0, 1):
        total = part[n, 1, own, :]
        for s in NEAR:
            slot = lax.rem(y + s, NY)
            arrived(recv_b.at[n, slot], b_s.at[n, 0], b_r.at[n, slot], at_y(s))
            total = total + recv_b[n, slot].astype(F32)
        if n == 0:
            values, slopes = gelu_parts(total)
            ah[0, at] = values.astype(BF)
        else:
            ah[1, at] = (total * slopes).astype(BF)
        for d in FAR:
            send(ah.at[n, at], ah.at[n, at], c_s.at[n, d], c_r.at[n, y], at_y(d))
        send(ah.at[n, at], ah.at[n, at], f_s.at[n, 0], f_r.at[n, y], other)
    for n in (0, 1):
        for s in NEAR:
            yy = lax.rem(y + s, NY)
            block = ah.at[n, k * NY + yy]
            arrived(block, c_s.at[n, 0], c_r.at[n, yy], at_y(s))
            send(block, block, f_s.at[n, s], f_r.at[n, yy], other)
        for s in (0,) + NEAR:
            yy = lax.rem(y + s, NY)
            arrived(ah.at[n, (1 - k) * NY + yy], f_s.at[n, 0], f_r.at[n, yy], other)
        weight, dims = ((down, NN), (up, NT))[n]
        prod[n] = dot(ah[n].reshape(256, ah.shape[3]), weight[...], dims)
        for s in (2, 1, 3, 0):
            p = lax.rem(z // 2 + s, NZ // 2)
            for e in (2, 1, 3):
                to = lax.rem(x + e, NX)
                for i in (0, 1):
                    rows = pl.ds(pl.multiple_of(p * 64 + i * 32 + to * 8, 8), 8)
                    send_x[n, to, 2 * p + i] = fold(prod[n, rows, :]).astype(BF)
                send(
                    send_x.at[n, to, pl.ds(2 * p, 2)], recv_x.at[n, x, pl.ds(2 * p, 2)],
                    dx_s.at[n, s, e], dx_r.at[n, x, p], at_x(e),
                )

    totals = []
    for n in (0, 1):
        for s in (2, 1, 3, 0):
            p = lax.rem(z // 2 + s, NZ // 2)
            for e in (1, 3, 2):
                xx = lax.rem(x + e, NX)
                arrived(recv_x.at[n, xx, pl.ds(2 * p, 2)], dx_s.at[n, 0, 0], dx_r.at[n, xx, p], at_x(e))
            for i in (0, 1):
                zz = 2 * p + i if s else (z + 1 - 2 * lax.rem(z, 2), z)[i]
                rows = pl.ds(pl.multiple_of(zz * 32 + x * 8, 8), 8)
                total = fold(prod[n, rows, :])
                for e in (1, 3, 2):
                    total = total + recv_x[n, lax.rem(x + e, NX), zz].astype(F32)
                if s or i == 0:
                    send_z[n, zz] = total.astype(BF)
                    send(send_z.at[n, zz], recv_z.at[n, z], dz_s.at[n, 2 * s + i], dz_r.at[n, z], (row, zz * NX + x))
        totals.append(total)
        if n == 0:
            ug_ref[...] = dot(xs[0], ah[1].reshape(256, ah.shape[3]), TN).astype(BF)
            dg_ref[...] = dot(ah[0].reshape(256, ah.shape[3]), xs[1], TN).astype(BF)
    for n in (0, 1):
        total = totals[n]
        for s in NEAR:
            slot = lax.rem(z + s, NZ)
            arrived(recv_z.at[n, slot], dz_s.at[n, 0], dz_r.at[n, slot], at_z(s))
            total = total + recv_z[n, slot].astype(F32)
        (lo_ref, ig_ref)[n][...] = unfold(total).astype(BF)
    for c in pending:
        c.wait_send()


def store(a, b, c, d, a_out, b_out, c_out, d_out, sems):
    copies = [
        pltpu.make_async_copy(src, dst, sems.at[i])
        for i, (src, dst) in enumerate(((c, c_out), (d, d_out), (a, a_out), (b, b_out)))
    ]
    for c in copies:
        c.start()
    for c in copies:
        c.wait()


def local(tokens, up_weight, down_weight, cotangent):
    w, h = up_weight.shape
    dma = pltpu.SemaphoreType.DMA
    vmem = pl.BlockSpec(memory_space=pltpu.VMEM)
    hbm = pl.BlockSpec(memory_space=pltpu.HBM)
    shapes = (
        jax.ShapeDtypeStruct((8, w), BF),
        jax.ShapeDtypeStruct((8, w), BF),
        jax.ShapeDtypeStruct((w, h), BF),
        jax.ShapeDtypeStruct((h, w), BF),
    )
    results = pl.pallas_call(
        kernel,
        out_shape=shapes,
        in_specs=[hbm] * 4,
        out_specs=(vmem,) * 4,
        scratch_shapes=[
            pltpu.VMEM((w, h), BF), pltpu.VMEM((h, w), BF),
            pltpu.VMEM((2, 8, w), BF),
            pltpu.VMEM((2, NX, NZ, 16, w // 2), BF),
            pltpu.VMEM((2, 256, w), BF),
            pltpu.VMEM((2, 2, 128, h), F32), pltpu.VMEM((2, 128, h), F32),
            pltpu.VMEM((2, NY, 16, h), BF), pltpu.VMEM((2, NY, 16, h), BF),
            pltpu.VMEM((2, 16, 16, h), BF),
            pltpu.VMEM((2, 256, w), F32),
            pltpu.VMEM((2, NX, NZ, 16, w // 2), BF), pltpu.VMEM((2, NX, NZ, 16, w // 2), BF),
            pltpu.VMEM((2, NZ, 16, w // 2), BF), pltpu.VMEM((2, NZ, 16, w // 2), BF),
            dma((4,)),
            dma((2, NZ)), dma((2, NZ)), dma((2, 4, NX)), dma((2, NX, 4)),
            dma((2,)), dma((2,)),
            dma((2, NY)), dma((2, NY)),
            dma((2, NY)), dma((2, NY)), dma((2, NY)), dma((2, NY)),
            dma((2, 4, NX)), dma((2, NX, 4)), dma((2, NZ)), dma((2, NZ)),
        ],
        compiler_params=pltpu.CompilerParams(
            collective_id=0, has_side_effects=True, vmem_limit_bytes=40 << 20
        ),
        cost_estimate=pl.CostEstimate(flops=1812000000, bytes_accessed=4800000, transcendentals=12288),
        name="sublayer",
    )(*(pltpu.with_memory_space_constraint(a, pltpu.HBM) for a in (tokens, cotangent, up_weight, down_weight)))
    return pl.pallas_call(
        store,
        out_shape=shapes,
        in_specs=[pl.BlockSpec(memory_space=pl.ANY)] * 4,
        out_specs=(hbm,) * 4,
        scratch_shapes=[dma((4,))],
        compiler_params=pltpu.CompilerParams(vmem_limit_bytes=4 << 20),
        name="store",
    )(*results)


def solution(mesh):
    in_specs = (P("col", "row"), P("row", "col"), P("col", "row"), P("col", "row"))
    out_specs = (P("col", "row"), P("col", "row"), P("row", "col"), P("col", "row"))
    return jax.shard_map(local, mesh=mesh, in_specs=in_specs, out_specs=out_specs, check_vma=False)
```

```python
import math

import jax
import jax.numpy as jnp
from jax import lax
from jax.experimental import pallas as pl
from jax.experimental.pallas import tpu as pltpu
from jax.sharding import PartitionSpec as P

coeff_cubic = 0.044715
root_ratio = math.sqrt(2.0 / math.pi)
MESH = pl.DeviceIdType.MESH
BF = jnp.bfloat16
F32 = jnp.float32

NY, NK, NZ, NX = 8, 2, 8, 4
NEAR = (1, 7, 2, 6, 3, 5, 4)
FAR = (4, 3, 5, 2, 6, 1, 7)


def gelu_parts(preact):
    inner = jnp.tanh(root_ratio * (preact + coeff_cubic * preact * preact * preact))
    values = 0.5 * preact * (1.0 + inner)
    slopes = 0.5 * (1.0 + inner) + 0.5 * preact * (1.0 - inner * inner) * root_ratio * (
        1.0 + 3.0 * coeff_cubic * preact * preact
    )
    return (values, slopes)


def dot(left, right, dims):
    return lax.dot_general(left, right, (dims, ((), ())), preferred_element_type=F32)


NN = ((1,), (0,))
NT = ((1,), (1,))
TN = ((0,), (0,))


def fold(block):
    half = block.shape[1] // 2
    return jnp.concatenate([block[:, :half], block[:, half:]], axis=0)


def unfold(block):
    return jnp.concatenate([block[:8], block[8:]], axis=1)


def kernel(
    tok_hbm, cot_hbm, up_hbm, down_hbm,
    lo_ref, ig_ref, ug_ref, dg_ref,
    up, down, shard, gat, xs, part, pair, send_b, recv_b, ah, hid, prod, send_x, recv_x, send_z, recv_z,
    wsem, az_s, ax_s, p_s, b_s, c_s, f_s, dx_s, dz_s,
    az_r, ax_r, p_r, b_r, c_r, f_r, dx_r, dz_r,
):
    row = lax.axis_index("row")
    col = lax.axis_index("col")
    y, k = row // NK, row % NK
    z, x = col // NX, col % NX

    def at_y(d):
        return (lax.rem(y + d, NY) * NK + k, col)

    def at_z(d):
        return (row, lax.rem(z + d, NZ) * NX + x)

    def at_x(d):
        return (row, z * NX + lax.rem(x + d, NX))

    other = (y * NK + 1 - k, col)

    def copy(src, dst, ss, rs, device):
        return pltpu.make_async_remote_copy(
            src_ref=src, dst_ref=dst, send_sem=ss, recv_sem=rs, device_id=device, device_id_type=MESH
        )

    def send(src, dst, ss, rs, device):
        copy(src, dst, ss, rs, device).start()

    def arrived(some, rs):
        copy(some, some, az_s, rs, other).wait_recv()

    load_tok = pltpu.make_async_copy(tok_hbm, shard.at[0], wsem.at[0])
    load_cot = pltpu.make_async_copy(cot_hbm, shard.at[1], wsem.at[1])
    load_up = pltpu.make_async_copy(up_hbm, up, wsem.at[2])
    load_down = pltpu.make_async_copy(down_hbm, down, wsem.at[3])
    load_tok.start()
    load_cot.start()
    load_up.start()
    load_down.start()

    barrier = pltpu.get_barrier_semaphore()
    peers = [at_y(d) for d in FAR] + [at_z(d) for d in FAR] + [at_x(d) for d in (2, 1, 3)] + [other]
    for device in peers:
        pl.semaphore_signal(barrier, inc=1, device_id=device, device_id_type=MESH)
    load_tok.wait()
    load_cot.wait()
    for n in (0, 1):
        gat[n, x, z] = fold(shard[n].astype(F32)).astype(BF)
    pl.semaphore_wait(barrier, len(peers))

    group = z // 4
    half = (1 - group, group)
    near = z // 2
    next_near = near + 1 - 2 * lax.rem(near, 2)
    mate = z + 1 - 2 * lax.rem(z, 2)
    chunks = ((2 * half[0], 2 * half[0] + 1), (next_near, near))

    def send_z_blocks(n):
        for d in FAR:
            send(gat.at[n, x, z], gat.at[n, x, z], az_s, az_r.at[n, near], at_z(d))

    def send_x_blocks(n, t):
        for j in (0, 1) if t == 0 else (1, 0):
            p = chunks[t][j]
            block = gat.at[n, x, pl.ds(2 * p, 2)]
            arrived(gat.at[n, x, mate] if (t, j) == (1, 1) else block, az_r.at[n, p])
            for d in (2, 1, 3):
                send(block, block, ax_s, ax_r.at[n, t], at_x(d))

    def rows_of(t):
        return pl.ds(pl.multiple_of(half[t] * 128, 128), 128)

    mine = pl.ds(pl.multiple_of(k * 64, 64), 64)
    theirs = pl.ds(pl.multiple_of((1 - k) * 64, 64), 64)
    loads = [load_up, load_down]

    def first_product(n, t):
        arrived(gat.at[n, pl.ds(0, 3), pl.ds(0, 4)], ax_r.at[n, t])
        blocks = [unfold(gat[n, j, half[t] * 4 + i].astype(F32)) for i in range(4) for j in range(NX)]
        block = jnp.concatenate(blocks, axis=0).astype(BF)
        xs[n, rows_of(t), :] = block
        if t == 0:
            loads[n].wait()
        weight, dims = ((up, NN), (down, NT))[n]
        c = 2 * n + t
        part[c] = dot(block, weight[...], dims)
        send(part.at[c, theirs], pair.at[c], p_s, p_r.at[c], other)

    own = pl.ds(pl.multiple_of(k * 64 + y * 8, 8), 8)

    def spread(n, t):
        c = 2 * n + t
        arrived(pair.at[c], p_r.at[c])
        for d in FAR + (0,):
            to = lax.rem(y + d, NY)
            rows = pl.ds(pl.multiple_of(k * 64 + to * 8, 8), 8)
            total = part[c, rows, :] + pair[c, pl.ds(pl.multiple_of(to * 8, 8), 8), :]
            if d:
                send_b[c, to] = fold(total).astype(BF)
                send(send_b.at[c, to], recv_b.at[c, y], b_s, b_r.at[c], at_y(d))
            else:
                part[c, rows, :] = total

    at = k * NY + y
    kept = [None, None]

    def middle(n, t):
        c = 2 * n + t
        total = fold(part[c, own, :])
        arrived(recv_b.at[c, pl.ds(0, NY - 1)], b_r.at[c])
        for s in NEAR:
            total = total + recv_b[c, lax.rem(y + s, NY)].astype(F32)
        if n == 0:
            values, kept[t] = gelu_parts(total)
            ah[c, at] = values.astype(BF)
        else:
            ah[c, at] = (total * kept[t]).astype(BF)
        for d in FAR:
            send(ah.at[c, at], ah.at[c, at], c_s, c_r.at[c], at_y(d))

    def forward(n, t):
        c = 2 * n + t
        arrived(ah.at[c, pl.ds(0, NY - 1)], c_r.at[c])
        block = ah.at[c, pl.ds(pl.multiple_of(k * NY, NY), NY)]
        send(block, block, f_s, f_r.at[c], other)

    def second_product(n, t):
        c = 2 * n + t
        arrived(ah.at[c, pl.ds(0, NY)], f_r.at[c])
        block = jnp.concatenate([unfold(ah[c, i].astype(F32)) for i in range(16)], axis=0).astype(BF)
        hid[n, rows_of(t), :] = block
        weight, dims = ((down, NN), (up, NT))[n]
        prod[c] = dot(block, weight[...], dims)
        for j in (0, 1):
            p = chunks[t][j]
            for e in (2, 1, 3):
                to = lax.rem(x + e, NX)
                for i in (0, 1):
                    rows = pl.ds(pl.multiple_of((p - 2 * half[t]) * 64 + i * 32 + to * 8, 8), 8)
                    send_x[n, to, 2 * p + i] = fold(prod[c, rows, :]).astype(BF)
                send(
                    send_x.at[n, to, pl.ds(2 * p, 2)], recv_x.at[n, x, pl.ds(2 * p, 2)],
                    dx_s, dx_r.at[n, p], at_x(e),
                )

    def combine(n, t):
        c = 2 * n + t
        for j in (0, 1):
            p = chunks[t][j]
            arrived(recv_x.at[n, pl.ds(0, 3), pl.ds(0, 2)], dx_r.at[n, p])
            for i in (0, 1):
                last = (t, j) == (1, 1)
                zz = (mate, z)[i] if last else 2 * p + i
                rows = pl.ds(pl.multiple_of((zz - 4 * half[t]) * 32 + x * 8, 8), 8)
                total = fold(prod[c, rows, :])
                for e in (1, 3, 2):
                    total = total + recv_x[n, lax.rem(x + e, NX), zz].astype(F32)
                if not (last and i):
                    send_z[n, zz] = total.astype(BF)
                    send(send_z.at[n, zz], recv_z.at[n, z], dz_s, dz_r.at[n], (row, zz * NX + x))
        return total

    def finish(n, total):
        arrived(recv_z.at[n, pl.ds(0, NZ - 1)], dz_r.at[n])
        for s in NEAR:
            total = total + recv_z[n, lax.rem(z + s, NZ)].astype(F32)
        (lo_ref, ig_ref)[n][...] = unfold(total).astype(BF)

    send_z_blocks(0)
    send_z_blocks(1)
    send_x_blocks(0, 0)
    send_x_blocks(0, 1)
    first_product(0, 0)
    send_x_blocks(1, 0)
    send_x_blocks(1, 1)
    spread(0, 0)
    first_product(0, 1)
    spread(0, 1)
    first_product(1, 0)
    spread(1, 0)
    first_product(1, 1)
    spread(1, 1)
    middle(0, 0)
    middle(0, 1)
    middle(1, 0)
    middle(1, 1)
    forward(0, 0)
    forward(0, 1)
    second_product(0, 0)
    forward(1, 0)
    second_product(0, 1)
    forward(1, 1)
    second_product(1, 0)
    second_product(1, 1)
    combine(0, 0)
    total = combine(0, 1)
    ug_ref[...] = dot(xs[0], hid[1], TN).astype(BF)
    dg_ref[...] = dot(hid[0], xs[1], TN).astype(BF)
    combine(1, 0)
    finish(0, total)
    total = combine(1, 1)
    finish(1, total)
    for sent, sem in (
        (gat.at[:, 0, pl.ds(0, 7)], az_s), (gat.at[:, pl.ds(0, 3)], ax_s), (pair, p_s),
        (send_b.at[:, pl.ds(0, 7)], b_s), (ah.at[:, pl.ds(0, 7)], c_s), (ah.at[:, pl.ds(0, 8)], f_s),
        (send_x.at[:, pl.ds(0, 3)], dx_s), (send_z.at[:, pl.ds(0, 7)], dz_s),
    ):
        copy(sent, sent, sem, dz_r.at[0], other).wait_send()


def store(a, b, c, d, a_out, b_out, c_out, d_out, sems):
    copies = [
        pltpu.make_async_copy(src, dst, sems.at[i])
        for i, (src, dst) in enumerate(((c, c_out), (d, d_out), (a, a_out), (b, b_out)))
    ]
    for c in copies:
        c.start()
    for c in copies:
        c.wait()


def local(tokens, up_weight, down_weight, cotangent):
    w, h = up_weight.shape
    dma = pltpu.SemaphoreType.DMA
    vmem = pl.BlockSpec(memory_space=pltpu.VMEM)
    hbm = pl.BlockSpec(memory_space=pltpu.HBM)
    shapes = (
        jax.ShapeDtypeStruct((8, w), BF),
        jax.ShapeDtypeStruct((8, w), BF),
        jax.ShapeDtypeStruct((w, h), BF),
        jax.ShapeDtypeStruct((h, w), BF),
    )
    results = pl.pallas_call(
        kernel,
        out_shape=shapes,
        in_specs=[hbm] * 4,
        out_specs=(vmem,) * 4,
        scratch_shapes=[
            pltpu.VMEM((w, h), BF), pltpu.VMEM((h, w), BF),
            pltpu.VMEM((2, 8, w), BF),
            pltpu.VMEM((2, NX, NZ, 16, w // 2), BF),
            pltpu.VMEM((2, 256, w), BF),
            pltpu.VMEM((4, 128, h), F32), pltpu.VMEM((4, 64, h), F32),
            pltpu.VMEM((4, NY, 16, h // 2), BF), pltpu.VMEM((4, NY, 16, h // 2), BF),
            pltpu.VMEM((4, 16, 16, h // 2), BF),
            pltpu.VMEM((2, 256, h), BF),
            pltpu.VMEM((4, 128, w), F32),
            pltpu.VMEM((2, NX, NZ, 16, w // 2), BF), pltpu.VMEM((2, NX, NZ, 16, w // 2), BF),
            pltpu.VMEM((2, NZ, 16, w // 2), BF), pltpu.VMEM((2, NZ, 16, w // 2), BF),
            dma((4,)),
            dma, dma, dma, dma, dma, dma, dma, dma,
            dma((2, 4)), dma((2, 2)), dma((4,)), dma((4,)), dma((4,)), dma((4,)), dma((2, 4)), dma((2,)),
        ],
        compiler_params=pltpu.CompilerParams(
            collective_id=0, has_side_effects=True, vmem_limit_bytes=40 << 20
        ),
        cost_estimate=pl.CostEstimate(flops=1812000000, bytes_accessed=4800000, transcendentals=12288),
        name="sublayer",
    )(*(pltpu.with_memory_space_constraint(a, pltpu.HBM) for a in (tokens, cotangent, up_weight, down_weight)))
    return pl.pallas_call(
        store,
        out_shape=shapes,
        in_specs=[pl.BlockSpec(memory_space=pl.ANY)] * 4,
        out_specs=(hbm,) * 4,
        scratch_shapes=[dma((4,))],
        compiler_params=pltpu.CompilerParams(vmem_limit_bytes=4 << 20),
        name="store",
    )(*results)


def solution(mesh):
    in_specs = (P("col", "row"), P("row", "col"), P("col", "row"), P("col", "row"))
    out_specs = (P("col", "row"), P("col", "row"), P("row", "col"), P("col", "row"))
    return jax.shard_map(local, mesh=mesh, in_specs=in_specs, out_specs=out_specs, check_vma=False)
```

```python
import math

import jax
import jax.numpy as jnp
from jax import lax
from jax.experimental import pallas as pl
from jax.experimental.pallas import tpu as pltpu
from jax.sharding import PartitionSpec as P

coeff_cubic = 0.044715
root_ratio = math.sqrt(2.0 / math.pi)
MESH = pl.DeviceIdType.MESH
BF = jnp.bfloat16
F32 = jnp.float32

NY, NK, NZ, NX = 8, 2, 8, 4
NEAR = (1, 7, 2, 6, 3, 5, 4)
FAR = (4, 3, 5, 2, 6, 1, 7)


def gelu_parts(preact):
    inner = jnp.tanh(root_ratio * (preact + coeff_cubic * preact * preact * preact))
    values = 0.5 * preact * (1.0 + inner)
    slopes = 0.5 * (1.0 + inner) + 0.5 * preact * (1.0 - inner * inner) * root_ratio * (
        1.0 + 3.0 * coeff_cubic * preact * preact
    )
    return (values, slopes)


def dot(left, right, dims):
    return lax.dot_general(left, right, (dims, ((), ())), preferred_element_type=F32)


NN = ((1,), (0,))
NT = ((1,), (1,))
TN = ((0,), (0,))


def fold(block):
    half = block.shape[1] // 2
    return jnp.concatenate([block[:, :half], block[:, half:]], axis=0)


def unfold(block):
    return jnp.concatenate([block[:8], block[8:]], axis=1)


def kernel(
    tok_hbm, cot_hbm, up_hbm, down_hbm,
    lo_ref, ig_ref, ug_ref, dg_ref,
    up, down, shard, gat, xs, part, pair, send_b, recv_b, ah, hid, prod, send_x, recv_x, send_z, recv_z,
    wsem, az_s, ax_s, ao_s, p_s, b_s, c_s, f_s, dx_s, dz_s,
    az_r, ax_r, ao_r, aw_r, p_r, b_r, c_r, f_r, dx_r, dz_r,
):
    row = lax.axis_index("row")
    col = lax.axis_index("col")
    y, k = row // NK, row % NK
    z, x = col // NX, col % NX

    def at_y(d):
        return (lax.rem(y + d, NY) * NK + k, col)

    def at_z(d):
        return (row, lax.rem(z + d, NZ) * NX + x)

    def at_x(d):
        return (row, z * NX + lax.rem(x + d, NX))

    other = (y * NK + 1 - k, col)

    def copy(src, dst, ss, rs, device):
        return pltpu.make_async_remote_copy(
            src_ref=src, dst_ref=dst, send_sem=ss, recv_sem=rs, device_id=device, device_id_type=MESH
        )

    def send(src, dst, ss, rs, device):
        copy(src, dst, ss, rs, device).start()

    def arrived(some, rs):
        copy(some, some, az_s, rs, other).wait_recv()

    load_tok = pltpu.make_async_copy(tok_hbm, shard.at[0], wsem.at[0])
    load_cot = pltpu.make_async_copy(cot_hbm, shard.at[1], wsem.at[1])
    load_up = pltpu.make_async_copy(up_hbm, up, wsem.at[2])
    load_down = pltpu.make_async_copy(down_hbm, down, wsem.at[3])
    load_tok.start()
    load_cot.start()
    load_up.start()
    load_down.start()

    barrier = pltpu.get_barrier_semaphore()
    peers = [at_y(d) for d in FAR] + [at_z(d) for d in FAR] + [at_x(d) for d in (2, 1, 3)] + [other]
    for device in peers:
        pl.semaphore_signal(barrier, inc=1, device_id=device, device_id_type=MESH)
    load_tok.wait()
    load_cot.wait()
    for n in (0, 1):
        gat[n, x, z] = fold(shard[n].astype(F32)).astype(BF)
    pl.semaphore_wait(barrier, len(peers))

    group = z // 4
    half = (1 - group, group)
    near = z // 2
    next_near = near + 1 - 2 * lax.rem(near, 2)
    mate = z + 1 - 2 * lax.rem(z, 2)
    chunks = ((2 * half[0], 2 * half[0] + 1), (next_near, near))

    across = lax.rem(x + 2, NX)
    sides = ((1, 3), (1, 3))

    def send_z_blocks(n):
        for d in FAR:
            send(gat.at[n, x, z], gat.at[n, x, z], az_s, az_r.at[n, near], at_z(d))

    def send_across(n):
        send(gat.at[n, x, z], gat.at[n, x, z], ao_s, ao_r.at[n], at_x(2))

    def send_far_blocks(n):
        block = gat.at[n, across, z]
        arrived(block, ao_r.at[n])
        for d in FAR:
            same = lax.rem(lax.rem(z + d, NZ) // 4 + group + 1, 2)
            send(block, block, az_s, aw_r.at[n, same], at_z(d))

    def send_x_blocks(n, t):
        for j in (0, 1) if t == 0 else (1, 0):
            p = chunks[t][j]
            block = gat.at[n, x, pl.ds(2 * p, 2)]
            arrived(gat.at[n, x, mate] if (t, j) == (1, 1) else block, az_r.at[n, p])
            for d in sides[n]:
                send(block, block, ax_s, ax_r.at[n, t], at_x(d))

    def rows_of(t):
        return pl.ds(pl.multiple_of(half[t] * 128, 128), 128)

    mine = pl.ds(pl.multiple_of(k * 64, 64), 64)
    theirs = pl.ds(pl.multiple_of((1 - k) * 64, 64), 64)
    loads = [load_up, load_down]

    def first_product(n, t):
        arrived(gat.at[n, pl.ds(0, len(sides[n])), pl.ds(0, 4)], ax_r.at[n, t])
        if len(sides[n]) == 2:
            arrived(gat.at[n, 0, pl.ds(0, 4 - t)], aw_r.at[n, t])
        blocks = [unfold(gat[n, j, half[t] * 4 + i].astype(F32)) for i in range(4) for j in range(NX)]
        block = jnp.concatenate(blocks, axis=0).astype(BF)
        xs[n, rows_of(t), :] = block
        if t == 0:
            loads[n].wait()
        weight, dims = ((up, NN), (down, NT))[n]
        c = 2 * n + t
        part[c] = dot(block, weight[...], dims)
        send(part.at[c, theirs], pair.at[c], p_s, p_r.at[c], other)

    own = pl.ds(pl.multiple_of(k * 64 + y * 8, 8), 8)

    def spread(n, t):
        c = 2 * n + t
        arrived(pair.at[c], p_r.at[c])
        for d in FAR + (0,):
            to = lax.rem(y + d, NY)
            rows = pl.ds(pl.multiple_of(k * 64 + to * 8, 8), 8)
            total = part[c, rows, :] + pair[c, pl.ds(pl.multiple_of(to * 8, 8), 8), :]
            if d:
                send_b[c, to] = fold(total).astype(BF)
                send(send_b.at[c, to], recv_b.at[c, y], b_s, b_r.at[c], at_y(d))
            else:
                part[c, rows, :] = total

    at = k * NY + y
    kept = [None, None]

    def middle(n, t):
        c = 2 * n + t
        total = fold(part[c, own, :])
        arrived(recv_b.at[c, pl.ds(0, NY - 1)], b_r.at[c])
        for s in NEAR:
            total = total + recv_b[c, lax.rem(y + s, NY)].astype(F32)
        if n == 0:
            values, kept[t] = gelu_parts(total)
            ah[c, at] = values.astype(BF)
        else:
            ah[c, at] = (total * kept[t]).astype(BF)
        for d in FAR:
            send(ah.at[c, at], ah.at[c, at], c_s, c_r.at[c], at_y(d))

    def forward(n, t):
        c = 2 * n + t
        arrived(ah.at[c, pl.ds(0, NY - 1)], c_r.at[c])
        block = ah.at[c, pl.ds(pl.multiple_of(k * NY, NY), NY)]
        send(block, block, f_s, f_r.at[c], other)

    def second_product(n, t):
        c = 2 * n + t
        arrived(ah.at[c, pl.ds(0, NY)], f_r.at[c])
        block = jnp.concatenate([unfold(ah[c, i].astype(F32)) for i in range(16)], axis=0).astype(BF)
        hid[n, rows_of(t), :] = block
        weight, dims = ((down, NN), (up, NT))[n]
        prod[c] = dot(block, weight[...], dims)
        for j in (0, 1):
            p = chunks[t][j]
            for e in (2, 1, 3):
                to = lax.rem(x + e, NX)
                for i in (0, 1):
                    rows = pl.ds(pl.multiple_of((p - 2 * half[t]) * 64 + i * 32 + to * 8, 8), 8)
                    send_x[n, to, 2 * p + i] = fold(prod[c, rows, :]).astype(BF)
                send(
                    send_x.at[n, to, pl.ds(2 * p, 2)], recv_x.at[n, x, pl.ds(2 * p, 2)],
                    dx_s, dx_r.at[n, p], at_x(e),
                )

    def combine(n, t):
        c = 2 * n + t
        for j in (0, 1):
            p = chunks[t][j]
            arrived(recv_x.at[n, pl.ds(0, 3), pl.ds(0, 2)], dx_r.at[n, p])
            for i in (0, 1):
                last = (t, j) == (1, 1)
                zz = (mate, z)[i] if last else 2 * p + i
                rows = pl.ds(pl.multiple_of((zz - 4 * half[t]) * 32 + x * 8, 8), 8)
                total = fold(prod[c, rows, :])
                for e in (1, 3, 2):
                    total = total + recv_x[n, lax.rem(x + e, NX), zz].astype(F32)
                if not (last and i):
                    send_z[n, zz] = total.astype(BF)
                    send(send_z.at[n, zz], recv_z.at[n, z], dz_s, dz_r.at[n], (row, zz * NX + x))
        return total

    def finish(n, total):
        arrived(recv_z.at[n, pl.ds(0, NZ - 1)], dz_r.at[n])
        for s in NEAR:
            total = total + recv_z[n, lax.rem(z + s, NZ)].astype(F32)
        (lo_ref, ig_ref)[n][...] = unfold(total).astype(BF)

    send_across(0)
    send_z_blocks(0)
    send_across(1)
    send_z_blocks(1)
    send_far_blocks(0)
    send_x_blocks(0, 0)
    send_x_blocks(0, 1)
    send_far_blocks(1)
    send_x_blocks(1, 0)
    send_x_blocks(1, 1)
    first_product(0, 0)
    spread(0, 0)
    first_product(0, 1)
    spread(0, 1)
    first_product(1, 0)
    spread(1, 0)
    first_product(1, 1)
    spread(1, 1)
    middle(0, 0)
    middle(0, 1)
    middle(1, 0)
    middle(1, 1)
    forward(0, 0)
    forward(0, 1)
    second_product(0, 0)
    second_product(0, 1)
    forward(1, 0)
    forward(1, 1)
    second_product(1, 0)
    second_product(1, 1)
    combine(0, 0)
    last01 = combine(0, 1)
    combine(1, 0)
    ug_ref[...] = dot(xs[0], hid[1], TN).astype(BF)
    dg_ref[...] = dot(hid[0], xs[1], TN).astype(BF)
    finish(0, last01)
    last11 = combine(1, 1)
    finish(1, last11)
    for sent, sem in (
        (gat.at[:, pl.ds(0, 2), pl.ds(0, 7)], az_s), (gat.at[:, pl.ds(0, 2)], ax_s),
        (gat.at[0, 0, pl.ds(0, 2)], ao_s), (pair, p_s),
        (send_b.at[:, pl.ds(0, 7)], b_s), (ah.at[:, pl.ds(0, 7)], c_s), (ah.at[:, pl.ds(0, 8)], f_s),
        (send_x.at[:, pl.ds(0, 3)], dx_s), (send_z.at[:, pl.ds(0, 7)], dz_s),
    ):
        copy(sent, sent, sem, dz_r.at[0], other).wait_send()


def store(a, b, c, d, a_out, b_out, c_out, d_out, sems):
    copies = [
        pltpu.make_async_copy(src, dst, sems.at[i])
        for i, (src, dst) in enumerate(((c, c_out), (d, d_out), (a, a_out), (b, b_out)))
    ]
    for c in copies:
        c.start()
    for c in copies:
        c.wait()


def local(tokens, up_weight, down_weight, cotangent):
    w, h = up_weight.shape
    dma = pltpu.SemaphoreType.DMA
    vmem = pl.BlockSpec(memory_space=pltpu.VMEM)
    hbm = pl.BlockSpec(memory_space=pltpu.HBM)
    shapes = (
        jax.ShapeDtypeStruct((8, w), BF),
        jax.ShapeDtypeStruct((8, w), BF),
        jax.ShapeDtypeStruct((w, h), BF),
        jax.ShapeDtypeStruct((h, w), BF),
    )
    results = pl.pallas_call(
        kernel,
        out_shape=shapes,
        in_specs=[hbm] * 4,
        out_specs=(vmem,) * 4,
        scratch_shapes=[
            pltpu.VMEM((w, h), BF), pltpu.VMEM((h, w), BF),
            pltpu.VMEM((2, 8, w), BF),
            pltpu.VMEM((2, NX, NZ, 16, w // 2), BF),
            pltpu.VMEM((2, 256, w), BF),
            pltpu.VMEM((4, 128, h), F32), pltpu.VMEM((4, 64, h), F32),
            pltpu.VMEM((4, NY, 16, h // 2), BF), pltpu.VMEM((4, NY, 16, h // 2), BF),
            pltpu.VMEM((4, 16, 16, h // 2), BF),
            pltpu.VMEM((2, 256, h), BF),
            pltpu.VMEM((4, 128, w), F32),
            pltpu.VMEM((2, NX, NZ, 16, w // 2), BF), pltpu.VMEM((2, NX, NZ, 16, w // 2), BF),
            pltpu.VMEM((2, NZ, 16, w // 2), BF), pltpu.VMEM((2, NZ, 16, w // 2), BF),
            dma((4,)),
            dma, dma, dma, dma, dma, dma, dma, dma, dma,
            dma((2, 4)), dma((2, 2)), dma((2,)), dma((2, 2)), dma((4,)), dma((4,)), dma((4,)), dma((4,)), dma((2, 4)), dma((2,)),
        ],
        compiler_params=pltpu.CompilerParams(
            collective_id=0, has_side_effects=True, vmem_limit_bytes=40 << 20
        ),
        cost_estimate=pl.CostEstimate(flops=1812000000, bytes_accessed=4800000, transcendentals=12288),
        name="sublayer",
    )(*(pltpu.with_memory_space_constraint(a, pltpu.HBM) for a in (tokens, cotangent, up_weight, down_weight)))
    return pl.pallas_call(
        store,
        out_shape=shapes,
        in_specs=[pl.BlockSpec(memory_space=pl.ANY)] * 4,
        out_specs=(hbm,) * 4,
        scratch_shapes=[dma((4,))],
        compiler_params=pltpu.CompilerParams(vmem_limit_bytes=4 << 20),
        name="store",
    )(*results)


def solution(mesh):
    in_specs = (P("col", "row"), P("row", "col"), P("col", "row"), P("col", "row"))
    out_specs = (P("col", "row"), P("col", "row"), P("row", "col"), P("col", "row"))
    return jax.shard_map(local, mesh=mesh, in_specs=in_specs, out_specs=out_specs, check_vma=False)
```

```python
import math

import jax
import jax.numpy as jnp
from jax import lax
from jax.experimental import pallas as pl
from jax.experimental.pallas import tpu as pltpu
from jax.sharding import PartitionSpec as P

coeff_cubic = 0.044715
root_ratio = math.sqrt(2.0 / math.pi)
MESH = pl.DeviceIdType.MESH
BF = jnp.bfloat16
F32 = jnp.float32

NY, NK, NZ, NX = 8, 2, 8, 4
NEAR = (1, 7, 2, 6, 3, 5, 4)
FAR = (4, 3, 5, 2, 6, 1, 7)


def gelu_parts(preact):
    inner = jnp.tanh(root_ratio * (preact + coeff_cubic * preact * preact * preact))
    values = 0.5 * preact * (1.0 + inner)
    slopes = 0.5 * (1.0 + inner) + 0.5 * preact * (1.0 - inner * inner) * root_ratio * (
        1.0 + 3.0 * coeff_cubic * preact * preact
    )
    return (values, slopes)


def dot(left, right, dims):
    return lax.dot_general(left, right, (dims, ((), ())), preferred_element_type=F32)


NN = ((1,), (0,))
NT = ((1,), (1,))
TN = ((0,), (0,))


def fold(block):
    half = block.shape[1] // 2
    return jnp.concatenate([block[:, :half], block[:, half:]], axis=0)


def unfold(block):
    return jnp.concatenate([block[:8], block[8:]], axis=1)


def kernel(
    tok_hbm, cot_hbm, up_hbm, down_hbm,
    lo_ref, ig_ref, ug_ref, dg_ref,
    up, down, shard, gat, xs, part, pair, send_b, recv_b, ah, hid, prod, send_x, recv_x, send_z, recv_z,
    wsem, az_s, ax_s, ao_s, p_s, b_s, c_s, f_s, dx_s, dz_s,
    az_r, ax_r, ao_r, aw_r, p_r, b_r, c_r, f_r, dx_r, dz_r,
):
    row = lax.axis_index("row")
    col = lax.axis_index("col")
    y, k = row // NK, row % NK
    z, x = col // NX, col % NX

    def at_y(d):
        return (lax.rem(y + d, NY) * NK + k, col)

    def at_z(d):
        return (row, lax.rem(z + d, NZ) * NX + x)

    def at_x(d):
        return (row, z * NX + lax.rem(x + d, NX))

    other = (y * NK + 1 - k, col)

    def copy(src, dst, ss, rs, device):
        return pltpu.make_async_remote_copy(
            src_ref=src, dst_ref=dst, send_sem=ss, recv_sem=rs, device_id=device, device_id_type=MESH
        )

    def send(src, dst, ss, rs, device):
        copy(src, dst, ss, rs, device).start()

    def arrived(some, rs):
        copy(some, some, az_s, rs, other).wait_recv()

    barrier = pltpu.get_barrier_semaphore()
    peers = [at_y(d) for d in FAR] + [at_z(d) for d in FAR] + [at_x(d) for d in (2, 1, 3)] + [other]
    for device in peers:
        pl.semaphore_signal(barrier, inc=1, device_id=device, device_id_type=MESH)
    load_tok = pltpu.make_async_copy(tok_hbm, shard.at[0], wsem.at[0])
    load_cot = pltpu.make_async_copy(cot_hbm, shard.at[1], wsem.at[1])
    load_up = pltpu.make_async_copy(up_hbm, up, wsem.at[2])
    load_down = pltpu.make_async_copy(down_hbm, down, wsem.at[3])
    load_tok.start()
    load_cot.start()
    load_up.start()
    load_down.start()

    load_tok.wait()
    load_cot.wait()
    for n in (0, 1):
        gat[n, x, z] = fold(shard[n].astype(F32)).astype(BF)
    pl.semaphore_wait(barrier, len(peers))

    group = z // 4
    half = (1 - group, group)
    near = z // 2
    next_near = near + 1 - 2 * lax.rem(near, 2)
    mate = z + 1 - 2 * lax.rem(z, 2)
    chunks = ((2 * half[0], 2 * half[0] + 1), (next_near, near))

    across = lax.rem(x + 2, NX)
    sides = ((1, 3), (1, 3))

    def send_z_blocks(n):
        for d in FAR:
            send(gat.at[n, x, z], gat.at[n, x, z], az_s, az_r.at[n, near], at_z(d))

    def send_across(n):
        send(gat.at[n, x, z], gat.at[n, x, z], ao_s, ao_r.at[n], at_x(2))

    def send_far_blocks(n):
        block = gat.at[n, across, z]
        arrived(block, ao_r.at[n])
        for d in FAR:
            same = lax.rem(lax.rem(z + d, NZ) // 4 + group + 1, 2)
            send(block, block, az_s, aw_r.at[n, same], at_z(d))

    def send_x_blocks(n, t):
        for j in (0, 1) if t == 0 else (1, 0):
            p = chunks[t][j]
            block = gat.at[n, x, pl.ds(2 * p, 2)]
            arrived(gat.at[n, x, mate] if (t, j) == (1, 1) else block, az_r.at[n, p])
            for d in sides[n]:
                send(block, block, ax_s, ax_r.at[n, t], at_x(d))

    def rows_of(t):
        return pl.ds(pl.multiple_of(half[t] * 128, 128), 128)

    mine = pl.ds(pl.multiple_of(k * 64, 64), 64)
    theirs = pl.ds(pl.multiple_of((1 - k) * 64, 64), 64)
    loads = [load_up, load_down]

    def first_product(n, t):
        arrived(gat.at[n, pl.ds(0, len(sides[n])), pl.ds(0, 4)], ax_r.at[n, t])
        if len(sides[n]) == 2:
            arrived(gat.at[n, 0, pl.ds(0, 4 - t)], aw_r.at[n, t])
        blocks = [unfold(gat[n, j, half[t] * 4 + i].astype(F32)) for i in range(4) for j in range(NX)]
        block = jnp.concatenate(blocks, axis=0).astype(BF)
        xs[n, rows_of(t), :] = block
        if t == 0:
            loads[n].wait()
        weight, dims = ((up, NN), (down, NT))[n]
        c = 2 * n + t
        part[c] = dot(block, weight[...], dims)
        send(part.at[c, theirs], pair.at[c], p_s, p_r.at[c], other)

    own = pl.ds(pl.multiple_of(k * 64 + y * 8, 8), 8)

    def spread(n, t):
        c = 2 * n + t
        arrived(pair.at[c], p_r.at[c])
        for d in FAR + (0,):
            to = lax.rem(y + d, NY)
            rows = pl.ds(pl.multiple_of(k * 64 + to * 8, 8), 8)
            total = part[c, rows, :] + pair[c, pl.ds(pl.multiple_of(to * 8, 8), 8), :]
            if d:
                send_b[c, to] = fold(total).astype(BF)
                send(send_b.at[c, to], recv_b.at[c, y], b_s, b_r.at[c], at_y(d))
            else:
                part[c, rows, :] = total

    at = k * NY + y
    kept = [None, None]

    def middle(n, t):
        c = 2 * n + t
        total = fold(part[c, own, :])
        arrived(recv_b.at[c, pl.ds(0, NY - 1)], b_r.at[c])
        for s in NEAR:
            total = total + recv_b[c, lax.rem(y + s, NY)].astype(F32)
        if n == 0:
            values, kept[t] = gelu_parts(total)
            ah[c, at] = values.astype(BF)
        else:
            ah[c, at] = (total * kept[t]).astype(BF)
        for d in FAR:
            send(ah.at[c, at], ah.at[c, at], c_s, c_r.at[c], at_y(d))

    def forward(n, t):
        c = 2 * n + t
        arrived(ah.at[c, pl.ds(0, NY - 1)], c_r.at[c])
        block = ah.at[c, pl.ds(pl.multiple_of(k * NY, NY), NY)]
        send(block, block, f_s, f_r.at[c], other)

    def second_product(n, t):
        c = 2 * n + t
        arrived(ah.at[c, pl.ds(0, NY)], f_r.at[c])
        block = jnp.concatenate([unfold(ah[c, i].astype(F32)) for i in range(16)], axis=0).astype(BF)
        hid[n, rows_of(t), :] = block
        weight, dims = ((down, NN), (up, NT))[n]
        prod[c] = dot(block, weight[...], dims)
        for j in (0, 1):
            p = chunks[t][j]
            for e in (2, 1, 3):
                to = lax.rem(x + e, NX)
                for i in (0, 1):
                    rows = pl.ds(pl.multiple_of((p - 2 * half[t]) * 64 + i * 32 + to * 8, 8), 8)
                    send_x[n, to, 2 * p + i] = fold(prod[c, rows, :]).astype(BF)
                send(
                    send_x.at[n, to, pl.ds(2 * p, 2)], recv_x.at[n, x, pl.ds(2 * p, 2)],
                    dx_s, dx_r.at[n, p], at_x(e),
                )

    def combine(n, t):
        c = 2 * n + t
        for j in (0, 1):
            p = chunks[t][j]
            arrived(recv_x.at[n, pl.ds(0, 3), pl.ds(0, 2)], dx_r.at[n, p])
            for i in (0, 1):
                last = (t, j) == (1, 1)
                zz = (mate, z)[i] if last else 2 * p + i
                rows = pl.ds(pl.multiple_of((zz - 4 * half[t]) * 32 + x * 8, 8), 8)
                total = fold(prod[c, rows, :])
                for e in (1, 3, 2):
                    total = total + recv_x[n, lax.rem(x + e, NX), zz].astype(F32)
                if not (last and i):
                    send_z[n, zz] = total.astype(BF)
                    send(send_z.at[n, zz], recv_z.at[n, z], dz_s, dz_r.at[n], (row, zz * NX + x))
        return total

    def finish(n, total):
        arrived(recv_z.at[n, pl.ds(0, NZ - 1)], dz_r.at[n])
        for s in NEAR:
            total = total + recv_z[n, lax.rem(z + s, NZ)].astype(F32)
        (lo_ref, ig_ref)[n][...] = unfold(total).astype(BF)

    send_across(0)
    send_z_blocks(0)
    send_across(1)
    send_z_blocks(1)
    send_far_blocks(0)
    send_x_blocks(0, 0)
    send_x_blocks(0, 1)
    send_far_blocks(1)
    send_x_blocks(1, 0)
    send_x_blocks(1, 1)
    first_product(0, 0)
    spread(0, 0)
    first_product(0, 1)
    spread(0, 1)
    first_product(1, 0)
    spread(1, 0)
    first_product(1, 1)
    spread(1, 1)
    middle(0, 0)
    middle(0, 1)
    middle(1, 0)
    middle(1, 1)
    forward(0, 0)
    second_product(0, 0)
    forward(0, 1)
    second_product(0, 1)
    forward(1, 0)
    second_product(1, 0)
    forward(1, 1)
    second_product(1, 1)
    combine(0, 0)
    last01 = combine(0, 1)
    combine(1, 0)
    last11 = combine(1, 1)
    ug_ref[...] = dot(xs[0], hid[1], TN).astype(BF)
    dg_ref[...] = dot(hid[0], xs[1], TN).astype(BF)
    finish(0, last01)
    finish(1, last11)
    for sent, sem in (
        (gat.at[:, pl.ds(0, 2), pl.ds(0, 7)], az_s), (gat.at[:, pl.ds(0, 2)], ax_s),
        (gat.at[0, 0, pl.ds(0, 2)], ao_s), (pair, p_s),
        (send_b.at[:, pl.ds(0, 7)], b_s), (ah.at[:, pl.ds(0, 7)], c_s), (ah.at[:, pl.ds(0, 8)], f_s),
        (send_x.at[:, pl.ds(0, 3)], dx_s), (send_z.at[:, pl.ds(0, 7)], dz_s),
    ):
        copy(sent, sent, sem, dz_r.at[0], other).wait_send()


def store(a, b, c, d, a_out, b_out, c_out, d_out, sems):
    copies = [
        pltpu.make_async_copy(src, dst, sems.at[i])
        for i, (src, dst) in enumerate(((c, c_out), (d, d_out), (a, a_out), (b, b_out)))
    ]
    for c in copies:
        c.start()
    for c in copies:
        c.wait()


def local(tokens, up_weight, down_weight, cotangent):
    w, h = up_weight.shape
    dma = pltpu.SemaphoreType.DMA
    vmem = pl.BlockSpec(memory_space=pltpu.VMEM)
    hbm = pl.BlockSpec(memory_space=pltpu.HBM)
    shapes = (
        jax.ShapeDtypeStruct((8, w), BF),
        jax.ShapeDtypeStruct((8, w), BF),
        jax.ShapeDtypeStruct((w, h), BF),
        jax.ShapeDtypeStruct((h, w), BF),
    )
    results = pl.pallas_call(
        kernel,
        out_shape=shapes,
        in_specs=[hbm] * 4,
        out_specs=(vmem,) * 4,
        scratch_shapes=[
            pltpu.VMEM((w, h), BF), pltpu.VMEM((h, w), BF),
            pltpu.VMEM((2, 8, w), BF),
            pltpu.VMEM((2, NX, NZ, 16, w // 2), BF),
            pltpu.VMEM((2, 256, w), BF),
            pltpu.VMEM((4, 128, h), F32), pltpu.VMEM((4, 64, h), F32),
            pltpu.VMEM((4, NY, 16, h // 2), BF), pltpu.VMEM((4, NY, 16, h // 2), BF),
            pltpu.VMEM((4, 16, 16, h // 2), BF),
            pltpu.VMEM((2, 256, h), BF),
            pltpu.VMEM((4, 128, w), F32),
            pltpu.VMEM((2, NX, NZ, 16, w // 2), BF), pltpu.VMEM((2, NX, NZ, 16, w // 2), BF),
            pltpu.VMEM((2, NZ, 16, w // 2), BF), pltpu.VMEM((2, NZ, 16, w // 2), BF),
            dma((4,)),
            dma, dma, dma, dma, dma, dma, dma, dma, dma,
            dma((2, 4)), dma((2, 2)), dma((2,)), dma((2, 2)), dma((4,)), dma((4,)), dma((4,)), dma((4,)), dma((2, 4)), dma((2,)),
        ],
        compiler_params=pltpu.CompilerParams(
            collective_id=0, has_side_effects=True, vmem_limit_bytes=40 << 20
        ),
        cost_estimate=pl.CostEstimate(flops=1812000000, bytes_accessed=4800000, transcendentals=12288),
        name="sublayer",
    )(*(pltpu.with_memory_space_constraint(a, pltpu.HBM) for a in (tokens, cotangent, up_weight, down_weight)))
    return pl.pallas_call(
        store,
        out_shape=shapes,
        in_specs=[pl.BlockSpec(memory_space=pl.ANY)] * 4,
        out_specs=(hbm,) * 4,
        scratch_shapes=[dma((4,))],
        compiler_params=pltpu.CompilerParams(vmem_limit_bytes=4 << 20),
        name="store",
    )(*results)


def solution(mesh):
    in_specs = (P("col", "row"), P("row", "col"), P("col", "row"), P("col", "row"))
    out_specs = (P("col", "row"), P("col", "row"), P("row", "col"), P("col", "row"))
    return jax.shard_map(local, mesh=mesh, in_specs=in_specs, out_specs=out_specs, check_vma=False)
```
